512 devices in a mesh: section: 32 (over y, z_lo, core), blk: 16 (over z_hi, x).
Axes of the slice: x: 4, y: 4, z: 16 (z_hi: 4, z_lo: 4; z = z_hi * 4 + z_lo), core: 2. Of those that a mesh axis runs over, the one named last changes fastest.
Arguments:
- sent_grad: bfloat16 [32, 2048, 3072], P('section', 'blk'), may hold values from -6 to 6
- gates: bfloat16 [32, 2048, 2], P('section', 'blk'), may hold values from 0.049804688 to 0.94921875
- slot_token: int32 [32, 256], P('section'), may hold values from 0 to 2048, as said below
- slot_rank: int32 [32, 256], P('section'), may hold values from 0 to 1
- pre_act: bfloat16 [32, 256, 2, 8192], P('section', None, None, 'blk'), may hold values from -6 to 6
- down_weight: bfloat16 [32, 8192, 3072], P('section', 'blk'), may hold values from -0.0625 to 0.0625
Outputs:
- d_pre: bfloat16 [32, 256, 2, 8192], P('section', None, None, 'blk')
- d_gate: float32 [32, 256], P('section')
The draws below stay inside these ranges and needn't reach their ends.
Inputs may be any that keep to these rules, and one draw needn't show every extreme that they name: `slot_token`: in every section the live slots come first and hold distinct tokens in ascending order; every later slot holds the pad value 2048. At most 32 slots of a section name tokens k * 128 to (k + 1) * 128 - 1 for any k, and in every section some k reaches that bound.
All inputs are finite; a program needn't handle non-finite values.
Results may differ from the reference program's by a relative error of at most 0.0029.
Values may be sent and summed in bfloat16 or wider, within the bound.
A program may use at most 64 MiB of HBM per device.

```python
import jax
import jax.numpy as jnp
from jax import lax

D = 3072
FF = 8192
TOK_DEV = 128
SLOTS = 256
TOKENS = 2048
SHARD_MOST = 32
SECTIONS = 32


def draw_slot_token(key, part):
    key = jax.random.fold_in(key, 7)
    key_count, key_full, key_score = jax.random.split(key, 3)
    cycle_size = TOKENS // TOK_DEV
    upper = max((SLOTS - SHARD_MOST) // max(cycle_size - 1, 1), 1)
    lower = max(upper // 3, 1)
    counts = jax.random.randint(key_count, (SECTIONS, cycle_size), lower, upper + 1)
    filled = jax.random.randint(key_full, (SECTIONS,), 0, cycle_size)
    counts = jnp.where(jnp.arange(cycle_size)[None, :] == filled[:, None], SHARD_MOST, counts)
    scores = jax.random.randint(key_score, (SECTIONS, cycle_size, TOK_DEV), 0, 2 ** 20) * TOK_DEV + jnp.arange(TOK_DEV)[None, None, :]
    order_rank = jnp.argsort(jnp.argsort(scores, axis=-1), axis=-1)
    chosen = order_rank < counts[:, :, None]
    token_grid = jnp.arange(TOKENS).reshape(1, cycle_size, TOK_DEV)
    keyed = jnp.where(chosen, token_grid, TOKENS + token_grid).reshape(SECTIONS, TOKENS)
    ordered = jnp.sort(keyed, axis=-1)[:, :SLOTS]
    return jnp.where(ordered < TOKENS, ordered, TOKENS).astype(jnp.int32)


def plant(drawn, stream_key, low, top_value):
    dims = drawn.shape
    spot = [jax.random.randint(jax.random.fold_in(stream_key, axis), (), 0, dims[axis]) for axis in range(len(dims))]
    drawn = drawn.at[tuple(spot)].set(low)
    longest = dims.index(max(dims))
    spot[longest] = (spot[longest] + 1) % dims[longest]
    return drawn.at[tuple(spot)].set(top_value)


def block_scale(stream_key, shape, cuts, smallest, top_value):
    factor_of = 1.0
    for axis_at, shards_of in cuts:
        steps = jax.random.uniform(jax.random.fold_in(jax.random.fold_in(stream_key, 6), axis_at), (shards_of,), jnp.float32, smallest / len(cuts), top_value / len(cuts))
        factor_of = factor_of * jnp.repeat(jnp.exp(steps), shape[axis_at] // shards_of).reshape((-1,) + (1,) * (len(shape) - 1 - axis_at))
    return factor_of


def gaussian(key, dims, width, bound, cuts=(), kind=jnp.bfloat16):
    array = width * jax.random.normal(key, dims, jnp.float32)
    if cuts:
        array = array * block_scale(key, dims, cuts, -0.22, 0.18)
    return jnp.clip(array, -bound, bound).astype(kind)


def setup_inputs(seed: int = 0) -> dict:
    splits = jax.random.split(jax.random.key(seed), 7)
    sent_grad = gaussian(splits[0], (SECTIONS, TOKENS, D), 1.0, 6.0, ((0, 32), (1, 16)))
    gates = jnp.clip(0.049804688 + 0.89941406 * jax.random.uniform(splits[1], (SECTIONS, TOKENS, 2), jnp.float32) ** block_scale(splits[1], (SECTIONS, TOKENS, 2), ((0, 32), (1, 16)), -0.2, 0.2), 0.049804688, 0.94921875).astype(jnp.bfloat16)
    slot_token = draw_slot_token(jax.random.fold_in(splits[6], 71), 0)
    slot_rank = plant(jax.random.randint(splits[3], (SECTIONS, SLOTS), 0, 2), jax.random.fold_in(splits[3], 1), 0, 1).astype(jnp.int32)
    pre_act = gaussian(splits[4], (SECTIONS, SLOTS, 2, FF), 1.0, 6.0, ((0, 32), (3, 16)))
    down_weight = gaussian(splits[5], (SECTIONS, FF, D), FF ** -0.5, 0.0625, ((0, 32), (1, 16)))
    return {"sent_grad": sent_grad, "gates": gates, "slot_token": slot_token, "slot_rank": slot_rank, "pre_act": pre_act, "down_weight": down_weight}


def one_section(operands):
    incoming, gate_table, tokens, slot_rank, pre, weight = operands
    is_live = tokens < TOKENS
    clamped = jnp.minimum(tokens, TOKENS - 1)
    slot_rows = jnp.where(is_live[:, None], incoming[clamped], jnp.zeros((), jnp.bfloat16))
    picked = gate_table[clamped].astype(jnp.float32)
    weight_of = jnp.where(is_live, jnp.where(slot_rank == 0, picked[:, 0], picked[:, 1]), jnp.zeros((), jnp.float32))
    dh_raw = jnp.dot(slot_rows, weight.T, preferred_element_type=jnp.float32)
    gate_pre = pre[:, 0, :].astype(jnp.float32)
    up_pre = pre[:, 1, :].astype(jnp.float32)
    sigmoid_gate = jax.nn.sigmoid(gate_pre)
    activated = gate_pre * sigmoid_gate
    hidden = lax.optimization_barrier((activated * up_pre).astype(jnp.bfloat16)).astype(jnp.float32)
    d_gate = jnp.sum(hidden * dh_raw, axis=1)
    grad_hidden = weight_of[:, None] * dh_raw
    d_up = grad_hidden * activated
    d_gp = grad_hidden * up_pre * sigmoid_gate * (1.0 + gate_pre * (1.0 - sigmoid_gate))
    d_pre = jnp.stack([d_gp, d_up], axis=1).astype(jnp.bfloat16)
    return d_pre, d_gate


def reference(sent_grad, gates, slot_token, slot_rank, pre_act, down_weight):
    incoming = jnp.roll(sent_grad, -1, axis=0)
    d_pre, d_gate = lax.map(one_section, (incoming, gates, slot_token, slot_rank, pre_act, down_weight))
    return (d_pre, d_gate)
```

```python
import functools

import jax
import jax.numpy as jnp
from jax import lax
from jax.experimental import pallas as pl
from jax.experimental.pallas import tpu as pltpu
from jax.sharding import PartitionSpec as P

MESH = pl.DeviceIdType.MESH
F32, BF16 = jnp.float32, jnp.bfloat16
NB = 16
GROUPS = 8
CHUNKS = 2
OFFSETS = (0, 3, 1, 2)


def iota(shape, dim):
    return lax.broadcasted_iota(jnp.int32, shape, dim)


def onehot(mask):
    return jnp.where(mask, 1.0, 0.0)


def dot(a, b, dims):
    return lax.dot_general(a, b, (dims, ((), ())), preferred_element_type=F32)


NN = ((1,), (0,))
NT = ((1,), (1,))


def relay_kernel(
    sections,
    tok_ref, rank_ref, gates_ref, rows_hbm, pre_hbm, w_hbm,
    dpre_ref, dgate_ref,
    x_v, w_v, pre_v, tokp_v, sb_v, r_v, g_v, wp_v, dg_v, pf_v, act_v, dgp_v, hid_v, dh_v,
    cp_sem, tok_sem, wp_send, wp_recv, a2a_send, a2a_recv, ag_send, ag_recv, dg_send, dg_recv,
):
    slots = tok_ref.shape[1]
    shard, width = x_v.shape
    units = w_v.shape[0]
    gw = width // GROUPS
    per = slots // NB
    s, b = lax.axis_index("section"), lax.axis_index("blk")
    h, x = b // 4, lax.rem(b, 4)
    up, down = lax.rem(s + 1, sections), lax.rem(s + sections - 1, sections)

    def at(dx, dh):
        return lax.rem(h + dh, 4) * 4 + lax.rem(x + dx, 4)

    copies = [
        pltpu.make_async_copy(src, dst, cp_sem.at[i])
        for i, (src, dst) in enumerate(((rows_hbm, x_v), (pre_hbm, pre_v), (w_hbm, w_v)))
    ]
    for copy in copies:
        copy.start()

    barrier = pltpu.get_barrier_semaphore()

    def greet(section, index):
        pl.semaphore_signal(barrier, inc=1, device_id=(section, index), device_id_type=MESH)

    greet(down, b)
    for i in range(NB):
        greet(up, lax.rem(b + i, NB))
    for i in range(1, NB):
        greet(s, lax.rem(b + i, NB))
    pl.semaphore_wait(barrier, 2 * NB)

    tok_copy = pltpu.make_async_remote_copy(
        tok_ref, tokp_v, tok_sem.at[0], tok_sem.at[1], device_id=(up, b), device_id_type=MESH
    )
    tok_copy.start()

    tokens = tok_ref[...]
    block = tokens // shard
    q = iota((slots, slots), 0)
    r = iota((slots, slots), 1)
    source = q // NB
    start = jnp.sum(onehot(block < source), axis=1, keepdims=True).astype(jnp.int32)
    later = jnp.where(r - start >= NB, 1, 0)
    found = onehot((block == source) & (later == lax.rem(q, 2))).astype(BF16)
    p = iota((GROUPS * per, slots), 0)
    wanted = onehot(iota((GROUPS * per, slots), 1) == lax.rem(p, per) * NB + b).astype(BF16)
    pack = dot(wanted, found, NT)
    same = (iota(pack.shape, 0) // per) == lax.rem(iota(pack.shape, 1), NB) // 2
    pack = jnp.where(same, pack, 0.0).astype(BF16)

    copies[0].wait()
    tok_copy.wait()
    tokens_below = tokp_v[...]
    first = jnp.sum(onehot(tokens_below < b * shard), axis=1, keepdims=True).astype(jnp.int32)
    later_below = jnp.where(r - first >= NB, 1, 0)
    owner = onehot((lax.rem(r, NB) == q // NB) & (later_below == lax.rem(q, 2))).astype(BF16)
    t = iota((shard, slots), 0)
    where_token = onehot(tokens_below - b * shard == t).astype(BF16)
    select = dot(owner, where_token, NT)
    group = lax.rem(iota(select.shape, 0), NB) // 2
    picked = jnp.zeros((slots, gw), F32)
    for g in range(GROUPS):
        mine = jnp.where(group == g, select, 0.0).astype(BF16)
        picked += dot(mine, x_v[:, g * gw:(g + 1) * gw], NN)
    sb_v[...] = picked.astype(BF16)

    a2a = []
    for i in range(NB):
        to = lax.rem(b + i, NB)
        copy = pltpu.make_async_remote_copy(
            sb_v.at[pl.ds(pl.multiple_of(to * NB, NB), NB)],
            r_v.at[pl.ds(pl.multiple_of(b * NB, NB), NB)],
            a2a_send.at[i], a2a_recv.at[i], device_id=(down, to), device_id_type=MESH,
        )
        copy.start()
        a2a.append(copy)

    here = onehot(tokens - b * shard == t).astype(BF16)
    both = dot(gates_ref[...], here, NN)
    part = jnp.where(rank_ref[...] == 0, both[0:1, :], both[1:2, :])
    wp_v[b] = jnp.broadcast_to(part, (8, slots))

    def exchange(buffer, send, recv):
        started = []
        for i in range(1, NB):
            copy = pltpu.make_async_remote_copy(
                buffer.at[b], buffer.at[b], send.at[i], recv.at[i],
                device_id=(s, lax.rem(b + i, NB)), device_id_type=MESH,
            )
            copy.start()
            started.append(copy)
        return started

    weights = exchange(wp_v, wp_send, wp_recv)

    copies[1].wait()
    pf_v[...] = pre_v[...].astype(F32)
    tiles = units // 128
    stride = NB * 2 * tiles
    for o in range(NB):
        for c in range(tiles):
            gate = pf_v[pl.ds(2 * tiles * o + 2 * c, per, stride=stride), :]
            up_pre = pf_v[pl.ds(2 * tiles * o + 2 * c + 1, per, stride=stride), :]
            sig = jax.nn.sigmoid(gate)
            activated = gate * sig
            into = (pl.ds(o * per, per), pl.ds(c * 128, 128))
            act_v[into] = activated
            dgp_v[into] = up_pre * sig * (1.0 + gate * (1.0 - sig))
            hid_v[into] = (activated * up_pre).astype(BF16).astype(F32)

    for copy in a2a:
        copy.wait_recv()
    rows = GROUPS * per // CHUNKS
    started = {}

    def send(name, chunk, owner_blk, part, to):
        low, size = chunk * rows, rows
        if part is not None:
            size = rows // 2
            low += part * size
        index = list(NAMES).index(name)
        ref = g_v.at[owner_blk, pl.ds(low, size)]
        copy = pltpu.make_async_remote_copy(
            ref, ref, ag_send.at[chunk * len(NAMES) + index], ag_recv.at[chunk * len(NAMES) + index],
            device_id=(s, to), device_id_type=MESH,
        )
        copy.start()
        started[name, chunk] = copy

    def arrived(name, chunk):
        started[name, chunk].wait_recv()

    def x_send(i, c):
        send(f"x+{i}", c, at(0, OFFSETS[i]), None, at(1, 0))
        send(f"x-{i}", c, at(0, OFFSETS[i]), None, at(3, 0))

    def x_forward(i, c):
        arrived(f"x+{i}", c)
        send(f"xf+{i}", c, at(3, OFFSETS[i]), 0, at(1, 0))
        arrived(f"x-{i}", c)
        send(f"xf-{i}", c, at(1, OFFSETS[i]), 1, at(3, 0))

    def z_forward(c):
        arrived("z+", c)
        send("zf+", c, at(0, 3), 0, at(0, 1))
        arrived("z-", c)
        send("zf-", c, at(0, 1), 1, at(0, 3))
        x_send(1, c)
        x_send(2, c)

    def z_last(c):
        arrived("zf+", c)
        arrived("zf-", c)
        x_send(3, c)

    dh_v[...] = jnp.zeros_like(dh_v)

    def multiply(c):
        for i in range(4):
            arrived(f"xf+{i}", c)
            arrived(f"xf-{i}", c)
        for g in range(c * GROUPS // CHUNKS, (c + 1) * GROUPS // CHUNKS):
            left = g_v[:, g * per:(g + 1) * per, :].reshape(slots, gw)
            dh_v[...] += dot(left, w_v[:, g * gw:(g + 1) * gw], NT)

    for c in range(CHUNKS):
        g_v[b, c * rows:(c + 1) * rows] = dot(pack[c * rows:(c + 1) * rows], r_v[...], NN).astype(BF16)
        send("z+", c, b, None, at(0, 1))
        send("z-", c, b, None, at(0, 3))
        x_send(0, c)
    for c in range(CHUNKS):
        x_forward(0, c)
    for copy in weights:
        copy.wait()
    weight_row = jnp.sum(jnp.sum(wp_v[...], axis=0)[0:1], axis=0, keepdims=True)
    in_place = r == lax.rem(q, per) * NB + q // per
    weight = jnp.sum(jnp.where(in_place, weight_row, 0.0), axis=1, keepdims=True)
    copies[2].wait()
    for c in range(CHUNKS):
        z_forward(c)
        if c:
            x_forward(1, c - 1)
            x_forward(2, c - 1)
    z_last(0)
    x_forward(1, CHUNKS - 1)
    x_forward(2, CHUNKS - 1)
    for c in range(1, CHUNKS):
        z_last(c)
        x_forward(3, c - 1)
    multiply(0)
    x_forward(3, CHUNKS - 1)
    for c in range(1, CHUNKS):
        multiply(c)

    dh = dh_v[...]
    share = jnp.sum(hid_v[...] * dh, axis=1, keepdims=True)
    dg_v[b] = jnp.broadcast_to(jnp.sum(jnp.where(in_place, share, 0.0), axis=0, keepdims=True), (8, slots))
    sums = exchange(dg_v, dg_send, dg_recv)

    grad = weight * dh
    d_gate_pre = grad * dgp_v[...]
    d_up = grad * act_v[...]
    for o in range(NB):
        for c in range(tiles):
            part = (slice(o * per, (o + 1) * per), slice(c * 128, (c + 1) * 128))
            pf_v[pl.ds(2 * tiles * o + 2 * c, per, stride=stride), :] = d_gate_pre[part]
            pf_v[pl.ds(2 * tiles * o + 2 * c + 1, per, stride=stride), :] = d_up[part]
    dpre_ref[...] = pf_v[...].astype(BF16)

    for copy in sums:
        copy.wait()
    total = dg_v[0]
    for i in range(1, NB):
        total += dg_v[i]
    dgate_ref[...] = total[0:1]

    tok_copy_done = [*a2a, *started.values()]
    for copy in tok_copy_done:
        copy.wait_send()


NAMES = ("z+", "z-", "zf+", "zf-") + tuple(
    f"{kind}{i}" for i in range(4) for kind in ("x+", "x-", "xf+", "xf-")
)


def per_device(sections, sent_grad, gates, slot_token, slot_rank, pre_act, down_weight):
    rows, weight = sent_grad[0], down_weight[0]
    shard, width = rows.shape
    slots, _, units = pre_act.shape[1:]
    tiles = units // 128
    gw, per = width // GROUPS, slots // NB
    pre = pre_act[0].reshape(slots, 2, tiles, 128).transpose(0, 2, 1, 3).reshape(slots * tiles * 2, 128)
    vmem = pl.BlockSpec(memory_space=pltpu.VMEM)
    hbm = pl.BlockSpec(memory_space=pl.ANY)
    dma = pltpu.SemaphoreType.DMA
    n_ag = CHUNKS * len(NAMES)
    d_pre, d_gate = pl.pallas_call(
        functools.partial(relay_kernel, sections),
        out_shape=(
            jax.ShapeDtypeStruct(pre.shape, BF16),
            jax.ShapeDtypeStruct((1, slots), F32),
        ),
        in_specs=[vmem, vmem, vmem, hbm, hbm, hbm],
        out_specs=(vmem, vmem),
        scratch_shapes=[
            pltpu.VMEM((shard, width), BF16),
            pltpu.VMEM(weight.shape, BF16),
            pltpu.VMEM(pre.shape, BF16),
            pltpu.VMEM((1, slots), jnp.int32),
            pltpu.VMEM((slots, gw), BF16),
            pltpu.VMEM((slots, gw), BF16),
            pltpu.VMEM((NB, GROUPS * per, gw), BF16),
            pltpu.VMEM((NB, 8, slots), F32),
            pltpu.VMEM((NB, 8, slots), F32),
            pltpu.VMEM(pre.shape, F32),
            pltpu.VMEM((slots, units), F32),
            pltpu.VMEM((slots, units), F32),
            pltpu.VMEM((slots, units), F32),
            pltpu.VMEM((slots, units), F32),
            dma((3,)), dma((2,)), dma((NB,)), dma((NB,)), dma((NB,)), dma((NB,)),
            dma((n_ag,)), dma((n_ag,)), dma((NB,)), dma((NB,)),
        ],
        compiler_params=pltpu.CompilerParams(
            collective_id=0, has_side_effects=True, vmem_limit_bytes=56 * 2**20
        ),
    )(slot_token, slot_rank, gates[0].T, rows, pre, weight)
    d_pre = d_pre.reshape(slots, tiles, 2, 128).transpose(0, 2, 1, 3).reshape(1, slots, 2, units)
    return d_pre, d_gate


def solution(mesh):
    placed = (
        P("section", "blk", None),
        P("section", "blk", None),
        P("section", None),
        P("section", None),
        P("section", None, None, "blk"),
        P("section", "blk", None),
    )
    return jax.shard_map(
        functools.partial(per_device, mesh.shape["section"]),
        mesh=mesh,
        in_specs=placed,
        out_specs=(P("section", None, None, "blk"), P("section", None)),
        check_vma=False,
    )
```

```python
import functools

import jax
import jax.numpy as jnp
from jax import lax
from jax.experimental import pallas as pl
from jax.experimental.pallas import tpu as pltpu
from jax.sharding import PartitionSpec as P

MESH = pl.DeviceIdType.MESH
F32, BF16 = jnp.float32, jnp.bfloat16
NB = 16
GROUPS = 8
CHUNKS = 3
OFFSETS = (0, 3, 1, 2)


def iota(shape, dim):
    return lax.broadcasted_iota(jnp.int32, shape, dim)


def onehot(mask):
    return jnp.where(mask, 1.0, 0.0)


def dot(a, b, dims):
    return lax.dot_general(a, b, (dims, ((), ())), preferred_element_type=F32)


NN = ((1,), (0,))
NT = ((1,), (1,))


def relay_kernel(
    sections,
    tok_hbm, rank_hbm, gates_hbm, rows_hbm, pre_hbm, w_hbm,
    dpre_hbm, dgate_hbm,
    tok_v, rank_v, gates_v, dpre_v, dsum_v, x_v, w_v, pre_v, tokp_v, sb_v, r_v, g_v, wp_v, dg_v, pf_v, act_v, dgp_v, hid_v, dh_v,
    far_sem, cp_sem, tok_sem, wp_send, wp_recv, a2a_send, a2a_recv, ag_send, ag_recv, dg_send, dg_recv,
):
    slots = tok_v.shape[1]
    shard, width = x_v.shape
    units = w_v.shape[0]
    cw = width // CHUNKS
    gw = cw // GROUPS
    per = slots // NB
    s, b = lax.axis_index("section"), lax.axis_index("blk")
    h, x = b // 4, lax.rem(b, 4)
    up, down = lax.rem(s + 1, sections), lax.rem(s + sections - 1, sections)

    def at(dx, dh):
        return lax.rem(h + dh, 4) * 4 + lax.rem(x + dx, 4)

    everyone = [at(dx, dh) for dh in (2, 3, 1, 0) for dx in (2, 1, 3, 0)]

    barrier = pltpu.get_barrier_semaphore()

    def greet(section, index):
        pl.semaphore_signal(barrier, inc=1, device_id=(section, index), device_id_type=MESH)

    greet(down, b)
    for dh in (3, 1, 0):
        for dx in range(4):
            greet(up, at(dx, dh))
            if dx or dh:
                greet(s, at(dx, dh))

    def load(index, src, dst):
        copy = pltpu.make_async_copy(src, dst, cp_sem.at[index])
        copy.start()
        return copy

    small = [load(0, tok_hbm, tok_v), load(1, rank_hbm, rank_v), load(2, gates_hbm, gates_v)]
    got_rows = load(3, rows_hbm, x_v)
    got_pre = load(4, pre_hbm, pre_v)
    got_w = load(5, w_hbm, w_v)
    pl.semaphore_wait(barrier, 24)

    tok_copy = pltpu.make_async_remote_copy(
        tok_hbm, tokp_v, tok_sem.at[0], tok_sem.at[1], device_id=(up, b), device_id_type=MESH
    )
    tok_copy.start()
    pl.semaphore_signal(far_sem, inc=1, device_id=(s, at(0, 3)), device_id_type=MESH)
    for copy in small:
        copy.wait()

    tokens = tok_v[...]
    block = tokens // shard
    q = iota((slots, slots), 0)
    r = iota((slots, slots), 1)
    source = q // NB
    start = jnp.sum(onehot(block < source), axis=1, keepdims=True).astype(jnp.int32)
    later = jnp.where(r - start >= NB, 1, 0)
    found = onehot((block == source) & (later == lax.rem(q, 2))).astype(BF16)
    p = iota((GROUPS * per, slots), 0)
    wanted = onehot(iota((GROUPS * per, slots), 1) == lax.rem(p, per) * NB + b).astype(BF16)
    pack = dot(wanted, found, NT)
    same = (iota(pack.shape, 0) // per) == lax.rem(iota(pack.shape, 1), NB) // 2
    pack = jnp.where(same, pack, 0.0).astype(BF16)

    got_rows.wait()
    tok_copy.wait()
    tokens_below = tokp_v[...]
    first = jnp.sum(onehot(tokens_below < b * shard), axis=1, keepdims=True).astype(jnp.int32)
    later_below = jnp.where(r - first >= NB, 1, 0)
    owner = onehot((lax.rem(r, NB) == q // NB) & (later_below == lax.rem(q, 2))).astype(BF16)
    t = iota((shard, slots), 0)
    where_token = onehot(tokens_below - b * shard == t).astype(BF16)
    select = dot(owner, where_token, NT)
    group = lax.rem(iota(select.shape, 0), NB) // 2
    select = jnp.concatenate([jnp.where(group == g, select, 0.0).astype(BF16) for g in range(GROUPS)], axis=1)
    a2a = []
    for c in range(CHUNKS):
        low = c * cw
        stacked = jnp.concatenate([x_v[:, low + g * gw:low + (g + 1) * gw] for g in range(GROUPS)], axis=0)
        sb_v[c] = dot(select, stacked, NN).astype(BF16)
        if c == 0:
            pl.semaphore_wait(far_sem, 1)
        for i, to in enumerate(everyone):
            copy = pltpu.make_async_remote_copy(
                sb_v.at[c, pl.ds(pl.multiple_of(to * NB, NB), NB)],
                r_v.at[c, pl.ds(pl.multiple_of(b * NB, NB), NB)],
                a2a_send.at[c * NB + i], a2a_recv.at[c * NB + i], device_id=(down, to), device_id_type=MESH,
            )
            copy.start()
            a2a.append(copy)

    here = onehot(tokens - b * shard == t).astype(BF16)
    both = dot(gates_v[...], here, NN)
    part = jnp.where(rank_v[...] == 0, both[0:1, :], both[1:2, :])
    wp_v[b] = part

    def exchange(buffer, send, recv):
        started = []
        for i, to in enumerate(everyone[:-1]):
            copy = pltpu.make_async_remote_copy(
                buffer.at[b], buffer.at[b], send.at[i], recv.at[i], device_id=(s, to), device_id_type=MESH
            )
            copy.start()
            started.append(copy)
        return started

    weights = exchange(wp_v, wp_send, wp_recv)

    got_pre.wait()
    pf_v[...] = pre_v[...].astype(F32)
    tiles = units // 128
    stride = NB * 2 * tiles
    for o in range(NB):
        for c in range(tiles):
            gate = pf_v[pl.ds(2 * tiles * o + 2 * c, per, stride=stride), :]
            up_pre = pf_v[pl.ds(2 * tiles * o + 2 * c + 1, per, stride=stride), :]
            sig = jax.nn.sigmoid(gate)
            activated = gate * sig
            into = (pl.ds(o * per, per), pl.ds(c * 128, 128))
            act_v[into] = activated
            dgp_v[into] = up_pre * sig * (1.0 + gate * (1.0 - sig))
            hid_v[into] = (activated * up_pre).astype(BF16).astype(F32)

    rows = GROUPS * per
    started = {}

    def send(name, chunk, owner_blk, part, to):
        low, size = (0, rows) if part is None else (part * rows // 2, rows // 2)
        index = list(NAMES).index(name)
        ref = g_v.at[chunk, owner_blk, pl.ds(low, size)]
        copy = pltpu.make_async_remote_copy(
            ref, ref, ag_send.at[chunk * len(NAMES) + index], ag_recv.at[chunk * len(NAMES) + index],
            device_id=(s, to), device_id_type=MESH,
        )
        copy.start()
        started[name, chunk] = copy

    def arrived(name, chunk):
        started[name, chunk].wait_recv()

    def x_send(i, c):
        send(f"x+{i}", c, at(0, OFFSETS[i]), None, at(1, 0))
        send(f"x-{i}", c, at(0, OFFSETS[i]), None, at(3, 0))
        send(f"xo{i}", c, at(0, OFFSETS[i]), None, at(2, 0))

    def z_forward(c):
        arrived("z+", c)
        send("zf+", c, at(0, 3), 0, at(0, 1))
        arrived("z-", c)
        send("zf-", c, at(0, 1), 1, at(0, 3))
        x_send(1, c)
        x_send(2, c)

    def z_last(c):
        arrived("zf+", c)
        arrived("zf-", c)
        x_send(3, c)

    def multiply(c):
        for i in range(4):
            for kind in ("x+", "x-", "xo"):
                arrived(f"{kind}{i}", c)
        left = [g_v[c, :, g * per:(g + 1) * per, :].reshape(slots, gw) for g in range(GROUPS)]
        product = dot(jnp.concatenate(left, axis=1), w_v[:, c * cw:(c + 1) * cw], NT)
        dh_v[...] = product if c == 0 else dh_v[...] + product

    for c in range(CHUNKS):
        for copy in a2a[c * NB:(c + 1) * NB]:
            copy.wait_recv()
        g_v[c, b] = dot(pack, r_v[c], NN).astype(BF16)
        send("z+", c, b, None, at(0, 1))
        send("z-", c, b, None, at(0, 3))
        x_send(0, c)
    z_forward(0)
    for copy in weights:
        copy.wait()
    weight_row = jnp.sum(wp_v[...], axis=0)
    in_place = r == lax.rem(q, per) * NB + q // per
    weight = jnp.sum(jnp.where(in_place, weight_row, 0.0), axis=1, keepdims=True)
    got_w.wait()
    for c in range(1, CHUNKS):
        z_forward(c)
    for c in range(CHUNKS):
        z_last(c)
    for c in range(CHUNKS):
        multiply(c)

    dh = dh_v[...]
    share = jnp.sum(hid_v[...] * dh, axis=1, keepdims=True)
    dg_v[b] = jnp.sum(jnp.where(in_place, share, 0.0), axis=0, keepdims=True)
    sums = exchange(dg_v, dg_send, dg_recv)

    grad = weight * dh
    d_gate_pre = grad * dgp_v[...]
    d_up = grad * act_v[...]
    for o in range(NB):
        for c in range(tiles):
            part = (slice(o * per, (o + 1) * per), slice(c * 128, (c + 1) * 128))
            pf_v[pl.ds(2 * tiles * o + 2 * c, per, stride=stride), :] = d_gate_pre[part]
            pf_v[pl.ds(2 * tiles * o + 2 * c + 1, per, stride=stride), :] = d_up[part]
    dpre_v[...] = pf_v[...].astype(BF16)
    put_pre = load(0, dpre_v, dpre_hbm)

    for copy in sums:
        copy.wait()
    total = dg_v[0]
    for i in range(1, NB):
        total += dg_v[i]
    dsum_v[...] = total
    put_gate = load(1, dsum_v, dgate_hbm)

    for copy in [*a2a, *started.values()]:
        copy.wait_send()
    put_pre.wait()
    put_gate.wait()


def hand_on_kernel(dpre_ref, dgate_ref, dpre_out, dgate_out):
    dpre_out[...] = dpre_ref[...]
    dgate_out[...] = dgate_ref[...]


NAMES = ("z+", "z-", "zf+", "zf-") + tuple(f"{kind}{i}" for i in range(4) for kind in ("x+", "x-", "xo"))


def per_device(sections, sent_grad, gates, slot_token, slot_rank, pre_act, down_weight):
    rows, weight = sent_grad[0], down_weight[0]
    shard, width = rows.shape
    slots, _, units = pre_act.shape[1:]
    tiles = units // 128
    gw, per = width // CHUNKS // GROUPS, slots // NB
    pre = pre_act[0].reshape(slots, 2, tiles, 128).transpose(0, 2, 1, 3).reshape(slots * tiles * 2, 128)
    vmem = pl.BlockSpec(memory_space=pltpu.VMEM)
    hbm = pl.BlockSpec(memory_space=pl.ANY)
    dma = pltpu.SemaphoreType.DMA
    n_ag = CHUNKS * len(NAMES)
    d_pre, d_gate = pl.pallas_call(
        functools.partial(relay_kernel, sections),
        out_shape=(
            jax.ShapeDtypeStruct(pre.shape, BF16),
            jax.ShapeDtypeStruct((1, slots), F32),
        ),
        in_specs=[hbm] * 6,
        out_specs=(hbm, hbm),
        scratch_shapes=[
            pltpu.VMEM((1, slots), jnp.int32),
            pltpu.VMEM((1, slots), jnp.int32),
            pltpu.VMEM((2, shard), BF16),
            pltpu.VMEM(pre.shape, BF16),
            pltpu.VMEM((1, slots), F32),
            pltpu.VMEM((shard, width), BF16),
            pltpu.VMEM(weight.shape, BF16),
            pltpu.VMEM(pre.shape, BF16),
            pltpu.VMEM((1, slots), jnp.int32),
            pltpu.VMEM((CHUNKS, slots, gw), BF16),
            pltpu.VMEM((CHUNKS, slots, gw), BF16),
            pltpu.VMEM((CHUNKS, NB, GROUPS * per, gw), BF16),
            pltpu.VMEM((NB, 1, slots), F32),
            pltpu.VMEM((NB, 1, slots), F32),
            pltpu.VMEM(pre.shape, F32),
            pltpu.VMEM((slots, units), F32),
            pltpu.VMEM((slots, units), F32),
            pltpu.VMEM((slots, units), F32),
            pltpu.VMEM((slots, units), F32),
            pltpu.SemaphoreType.REGULAR, dma((6,)), dma((2,)), dma((NB,)), dma((NB,)), dma((CHUNKS * NB,)), dma((CHUNKS * NB,)),
            dma((n_ag,)), dma((n_ag,)), dma((NB,)), dma((NB,)),
        ],
        compiler_params=pltpu.CompilerParams(
            collective_id=0, has_side_effects=True, vmem_limit_bytes=56 * 2**20
        ),
    )(slot_token, slot_rank, gates[0].T, rows, pre, weight)
    d_pre, d_gate = pl.pallas_call(
        hand_on_kernel,
        out_shape=(
            jax.ShapeDtypeStruct(pre.shape, BF16),
            jax.ShapeDtypeStruct((1, slots), F32),
        ),
        in_specs=[vmem, vmem],
        out_specs=(vmem, vmem),
    )(d_pre, d_gate)
    d_pre = d_pre.reshape(slots, tiles, 2, 128).transpose(0, 2, 1, 3).reshape(1, slots, 2, units)
    return d_pre, d_gate


def solution(mesh):
    placed = (
        P("section", "blk", None),
        P("section", "blk", None),
        P("section", None),
        P("section", None),
        P("section", None, None, "blk"),
        P("section", "blk", None),
    )
    return jax.shard_map(
        functools.partial(per_device, mesh.shape["section"]),
        mesh=mesh,
        in_specs=placed,
        out_specs=(P("section", None, None, "blk"), P("section", None)),
        check_vma=False,
    )
```

```python
import functools

import jax
import jax.numpy as jnp
from jax import lax
from jax.experimental import pallas as pl
from jax.experimental.pallas import tpu as pltpu
from jax.sharding import PartitionSpec as P

MESH = pl.DeviceIdType.MESH
F32, BF16 = jnp.float32, jnp.bfloat16
NB = 16
GROUPS = 8
CHUNKS = 3
OFFSETS = (0, 3, 1, 2)


def iota(shape, dim):
    return lax.broadcasted_iota(jnp.int32, shape, dim)


def onehot(mask):
    return jnp.where(mask, 1.0, 0.0)


def dot(a, b, dims):
    return lax.dot_general(a, b, (dims, ((), ())), preferred_element_type=F32)


NN = ((1,), (0,))
NT = ((1,), (1,))


def relay_kernel(
    sections,
    tok_hbm, rank_hbm, gates_hbm, rows_hbm, pre_hbm, w_hbm,
    dpre_hbm, dgate_hbm,
    place_v, tok_v, rank_v, gates_v, dpre_v, dsum_v, x_v, w_v, pre_v, tokp_v, sb_v, r_v, g_v, wp_v, dg_v, pf_v, act_v, dgp_v, hid_v, dh_v,
    far_sem, cp_sem, tok_sem, wp_send, wp_recv, a2a_send, a2a_recv, ag_send, ag_recv, dg_send, dg_recv,
):
    slots = tok_v.shape[1]
    shard, width = x_v.shape
    units = w_v.shape[0]
    cw = width // CHUNKS
    gw = cw // GROUPS
    per = slots // NB
    s, b = lax.axis_index("section"), lax.axis_index("blk")
    h, x = b // 4, lax.rem(b, 4)
    up, down = lax.rem(s + 1, sections), lax.rem(s + sections - 1, sections)

    def at(dx, dh):
        return lax.rem(h + dh, 4) * 4 + lax.rem(x + dx, 4)

    everyone = [at(dx, dh) for dh in (2, 3, 1, 0) for dx in (2, 1, 3, 0)]

    barrier = pltpu.get_barrier_semaphore()

    def greet(section, index):
        pl.semaphore_signal(barrier, inc=1, device_id=(section, index), device_id_type=MESH)

    greet(down, b)
    for dh in (3, 1, 0):
        for dx in range(4):
            if dx or dh:
                greet(s, at(dx, dh))

    def load(index, src, dst):
        copy = pltpu.make_async_copy(src, dst, cp_sem.at[index])
        copy.start()
        return copy

    small = [load(0, tok_hbm, tok_v), load(1, rank_hbm, rank_v), load(2, gates_hbm, gates_v)]
    got_rows = load(3, rows_hbm, x_v)
    got_pre = load(4, pre_hbm, pre_v)
    got_w = load(5, w_hbm, w_v)
    pl.semaphore_wait(barrier, 12)

    tok_copy = pltpu.make_async_remote_copy(
        tok_hbm, tokp_v, tok_sem.at[0], tok_sem.at[1], device_id=(up, b), device_id_type=MESH
    )
    tok_copy.start()

    got_rows.wait()
    tok_copy.wait()
    pl.semaphore_signal(far_sem, inc=1, device_id=(s, at(0, 3)), device_id_type=MESH)
    q = iota((slots, slots), 0)
    r = iota((slots, slots), 1)
    tokens_below = tokp_v[...]
    first = jnp.sum(onehot(tokens_below < b * shard), axis=1, keepdims=True).astype(jnp.int32)
    t = iota((shard, slots), 0)
    where_token = onehot(tokens_below - b * shard == t).astype(BF16)
    wide = iota((2 * NB, slots), 1)
    line = iota((2 * NB, slots), 0)
    later_below = jnp.where(wide - first >= NB, 1, 0)
    owner = onehot((lax.rem(wide, NB) == lax.rem(line, NB)) & (later_below == line // NB)).astype(BF16)
    select = dot(owner, where_token, NT).astype(BF16)
    a2a = {}

    def pick(c):
        picked = dot(select, x_v[:, c * cw:(c + 1) * cw], NN)
        for g in range(GROUPS):
            for k in range(2):
                place_v[pl.ds(2 * g + k, NB, stride=NB), :] = picked[k * NB:(k + 1) * NB, g * gw:(g + 1) * gw]
        sb_v[c] = place_v[...].astype(BF16)

    def deal(c, who):
        for i in who:
            to = everyone[i]
            copy = pltpu.make_async_remote_copy(
                sb_v.at[c, pl.ds(pl.multiple_of(to * NB, NB), NB)],
                r_v.at[c, pl.ds(pl.multiple_of(b * NB, NB), NB)],
                a2a_send.at[c * NB + i], a2a_recv.at[c * NB + i], device_id=(down, to), device_id_type=MESH,
            )
            copy.start()
            a2a[c, i] = copy

    far, near = range(4), range(4, NB)
    pick(0)
    for c in range(CHUNKS):
        pick(c)
        deal(c, near)
    pl.semaphore_wait(far_sem, 1)
    for c in range(CHUNKS):
        deal(c, far)

    for copy in small:
        copy.wait()
    tokens = tok_v[...]
    block = tokens // shard
    source = q // NB
    start = jnp.sum(onehot(block < source), axis=1, keepdims=True).astype(jnp.int32)
    later = jnp.where(r - start >= NB, 1, 0)
    found = onehot((block == source) & (later == lax.rem(q, 2))).astype(BF16)
    p = iota((GROUPS * per, slots), 0)
    wanted = onehot(iota((GROUPS * per, slots), 1) == lax.rem(p, per) * NB + b).astype(BF16)
    pack = dot(wanted, found, NT)
    same = (iota(pack.shape, 0) // per) == lax.rem(iota(pack.shape, 1), NB) // 2
    pack = jnp.where(same, pack, 0.0).astype(BF16)

    here = onehot(tokens - b * shard == t).astype(BF16)
    both = dot(gates_v[...], here, NN)
    part = jnp.where(rank_v[...] == 0, both[0:1, :], both[1:2, :])
    wp_v[b] = part

    def exchange(buffer, send, recv):
        started = []
        for i, to in enumerate(everyone[:-1]):
            copy = pltpu.make_async_remote_copy(
                buffer.at[b], buffer.at[b], send.at[i], recv.at[i], device_id=(s, to), device_id_type=MESH
            )
            copy.start()
            started.append(copy)
        return started

    weights = exchange(wp_v, wp_send, wp_recv)

    got_pre.wait()
    pf_v[...] = pre_v[...].astype(F32)
    tiles = units // 128
    stride = NB * 2 * tiles
    for o in range(NB):
        for c in range(tiles):
            gate = pf_v[pl.ds(2 * tiles * o + 2 * c, per, stride=stride), :]
            up_pre = pf_v[pl.ds(2 * tiles * o + 2 * c + 1, per, stride=stride), :]
            sig = jax.nn.sigmoid(gate)
            activated = gate * sig
            into = (pl.ds(o * per, per), pl.ds(c * 128, 128))
            act_v[into] = activated
            dgp_v[into] = up_pre * sig * (1.0 + gate * (1.0 - sig))
            hid_v[into] = (activated * up_pre).astype(BF16).astype(F32)

    rows = GROUPS * per
    started = {}

    def send(name, chunk, owner_blk, part, to):
        low, size = (0, rows) if part is None else (part * rows // 2, rows // 2)
        index = list(NAMES).index(name)
        ref = g_v.at[chunk, owner_blk, pl.ds(low, size)]
        copy = pltpu.make_async_remote_copy(
            ref, ref, ag_send.at[chunk * len(NAMES) + index], ag_recv.at[chunk * len(NAMES) + index],
            device_id=(s, to), device_id_type=MESH,
        )
        copy.start()
        started[name, chunk] = copy

    def arrived(name, chunk):
        started[name, chunk].wait_recv()

    def x_send(i, c):
        send(f"x+{i}", c, at(0, OFFSETS[i]), None, at(1, 0))
        send(f"x-{i}", c, at(0, OFFSETS[i]), None, at(3, 0))
        send(f"xo{i}", c, at(0, OFFSETS[i]), None, at(2, 0))

    def z_forward(c):
        arrived("z+", c)
        send("zf+", c, at(0, 3), 0, at(0, 1))
        arrived("z-", c)
        send("zf-", c, at(0, 1), 1, at(0, 3))
        x_send(1, c)
        x_send(2, c)

    def z_last(c):
        arrived("zf+", c)
        arrived("zf-", c)
        x_send(3, c)

    def multiply(c):
        for i in range(4):
            for kind in ("x+", "x-", "xo"):
                arrived(f"{kind}{i}", c)
        left = [g_v[c, :, g * per:(g + 1) * per, :].reshape(slots, gw) for g in range(GROUPS)]
        product = dot(jnp.concatenate(left, axis=1), w_v[:, c * cw:(c + 1) * cw], NT)
        dh_v[...] = product if c == 0 else dh_v[...] + product

    for c in range(CHUNKS):
        for i in range(NB):
            a2a[c, i].wait_recv()
        g_v[c, b] = dot(pack, r_v[c], NN).astype(BF16)
        send("z+", c, b, None, at(0, 1))
        send("z-", c, b, None, at(0, 3))
        x_send(0, c)
    z_forward(0)
    for copy in weights:
        copy.wait()
    weight_row = jnp.sum(wp_v[...], axis=0)
    in_place = r == lax.rem(q, per) * NB + q // per
    weight = jnp.sum(jnp.where(in_place, weight_row, 0.0), axis=1, keepdims=True)
    got_w.wait()
    for c in range(1, CHUNKS):
        z_forward(c)
    for c in range(CHUNKS):
        z_last(c)
    for c in range(CHUNKS):
        multiply(c)

    dh = dh_v[...]
    share = jnp.sum(hid_v[...] * dh, axis=1, keepdims=True)
    dg_v[b] = jnp.sum(jnp.where(in_place, share, 0.0), axis=0, keepdims=True)
    sums = exchange(dg_v, dg_send, dg_recv)

    grad = weight * dh
    d_gate_pre = grad * dgp_v[...]
    d_up = grad * act_v[...]
    for o in range(NB):
        for c in range(tiles):
            part = (slice(o * per, (o + 1) * per), slice(c * 128, (c + 1) * 128))
            pf_v[pl.ds(2 * tiles * o + 2 * c, per, stride=stride), :] = d_gate_pre[part]
            pf_v[pl.ds(2 * tiles * o + 2 * c + 1, per, stride=stride), :] = d_up[part]
    dpre_v[...] = pf_v[...].astype(BF16)
    put_pre = load(0, dpre_v, dpre_hbm)

    for copy in sums:
        copy.wait()
    total = dg_v[0]
    for i in range(1, NB):
        total += dg_v[i]
    dsum_v[...] = total
    put_gate = load(1, dsum_v, dgate_hbm)

    for copy in [*a2a.values(), *started.values()]:
        copy.wait_send()
    put_pre.wait()
    put_gate.wait()


def hand_on_kernel(dpre_ref, dgate_ref, dpre_out, dgate_out):
    dpre_out[...] = dpre_ref[...]
    dgate_out[...] = dgate_ref[...]


NAMES = ("z+", "z-", "zf+", "zf-") + tuple(f"{kind}{i}" for i in range(4) for kind in ("x+", "x-", "xo"))


def per_device(sections, sent_grad, gates, slot_token, slot_rank, pre_act, down_weight):
    rows, weight = sent_grad[0], down_weight[0]
    shard, width = rows.shape
    slots, _, units = pre_act.shape[1:]
    tiles = units // 128
    gw, per = width // CHUNKS // GROUPS, slots // NB
    pre = pre_act[0].reshape(slots, 2, tiles, 128).transpose(0, 2, 1, 3).reshape(slots * tiles * 2, 128)
    vmem = pl.BlockSpec(memory_space=pltpu.VMEM)
    hbm = pl.BlockSpec(memory_space=pl.ANY)
    dma = pltpu.SemaphoreType.DMA
    n_ag = CHUNKS * len(NAMES)
    d_pre, d_gate = pl.pallas_call(
        functools.partial(relay_kernel, sections),
        out_shape=(
            jax.ShapeDtypeStruct(pre.shape, BF16),
            jax.ShapeDtypeStruct((1, slots), F32),
        ),
        in_specs=[hbm] * 6,
        out_specs=(hbm, hbm),
        scratch_shapes=[
            pltpu.VMEM((slots, gw), F32),
            pltpu.VMEM((1, slots), jnp.int32),
            pltpu.VMEM((1, slots), jnp.int32),
            pltpu.VMEM((2, shard), BF16),
            pltpu.VMEM(pre.shape, BF16),
            pltpu.VMEM((1, slots), F32),
            pltpu.VMEM((shard, width), BF16),
            pltpu.VMEM(weight.shape, BF16),
            pltpu.VMEM(pre.shape, BF16),
            pltpu.VMEM((1, slots), jnp.int32),
            pltpu.VMEM((CHUNKS, slots, gw), BF16),
            pltpu.VMEM((CHUNKS, slots, gw), BF16),
            pltpu.VMEM((CHUNKS, NB, GROUPS * per, gw), BF16),
            pltpu.VMEM((NB, 1, slots), F32),
            pltpu.VMEM((NB, 1, slots), F32),
            pltpu.VMEM(pre.shape, F32),
            pltpu.VMEM((slots, units), F32),
            pltpu.VMEM((slots, units), F32),
            pltpu.VMEM((slots, units), F32),
            pltpu.VMEM((slots, units), F32),
            pltpu.SemaphoreType.REGULAR, dma((6,)), dma((2,)), dma((NB,)), dma((NB,)), dma((CHUNKS * NB,)), dma((CHUNKS * NB,)),
            dma((n_ag,)), dma((n_ag,)), dma((NB,)), dma((NB,)),
        ],
        compiler_params=pltpu.CompilerParams(
            collective_id=0, has_side_effects=True, vmem_limit_bytes=56 * 2**20
        ),
    )(slot_token, slot_rank, gates[0].T, rows, pre, weight)
    d_pre, d_gate = pl.pallas_call(
        hand_on_kernel,
        out_shape=(
            jax.ShapeDtypeStruct(pre.shape, BF16),
            jax.ShapeDtypeStruct((1, slots), F32),
        ),
        in_specs=[vmem, vmem],
        out_specs=(vmem, vmem),
    )(d_pre, d_gate)
    d_pre = d_pre.reshape(slots, tiles, 2, 128).transpose(0, 2, 1, 3).reshape(1, slots, 2, units)
    return d_pre, d_gate


def solution(mesh):
    placed = (
        P("section", "blk", None),
        P("section", "blk", None),
        P("section", None),
        P("section", None),
        P("section", None, None, "blk"),
        P("section", "blk", None),
    )
    return jax.shard_map(
        functools.partial(per_device, mesh.shape["section"]),
        mesh=mesh,
        in_specs=placed,
        out_specs=(P("section", None, None, "blk"), P("section", None)),
        check_vma=False,
    )
```

```python
import functools

import jax
import jax.numpy as jnp
from jax import lax
from jax.experimental import pallas as pl
from jax.experimental.pallas import tpu as pltpu
from jax.sharding import PartitionSpec as P

MESH = pl.DeviceIdType.MESH
F32, BF16 = jnp.float32, jnp.bfloat16
NB = 16
GROUPS = 8
CHUNKS = 3
OFFSETS = (0, 3, 1, 2)


def iota(shape, dim):
    return lax.broadcasted_iota(jnp.int32, shape, dim)


def onehot(mask):
    return jnp.where(mask, 1.0, 0.0)


def dot(a, b, dims):
    return lax.dot_general(a, b, (dims, ((), ())), preferred_element_type=F32)


NN = ((1,), (0,))
NT = ((1,), (1,))


def relay_kernel(
    sections,
    tok_hbm, rank_hbm, gates_hbm, rows_hbm, pre_hbm, w_hbm,
    dpre_hbm, dgate_hbm,
    place_v, tok_v, rank_v, gates_v, dpre_v, dsum_v, x_v, w_v, pre_v, tokp_v, sb_v, r_v, g_v, wp_v, dg_v, pf_v, act_v, dgp_v, hid_v, dh_v,
    far_sem, cp_sem, tok_sem, wp_send, wp_recv, a2a_send, a2a_recv, ag_send, ag_recv, dg_send, dg_recv,
):
    slots = tok_v.shape[1]
    shard, width = x_v.shape
    units = w_v.shape[0]
    cw = width // CHUNKS
    gw = cw // GROUPS
    per = slots // NB
    s, b = lax.axis_index("section"), lax.axis_index("blk")
    h, x = b // 4, lax.rem(b, 4)
    up, down = lax.rem(s + 1, sections), lax.rem(s + sections - 1, sections)

    def at(dx, dh):
        return lax.rem(h + dh, 4) * 4 + lax.rem(x + dx, 4)

    everyone = [at(dx, dh) for dh in (2, 3, 1, 0) for dx in (2, 1, 3, 0)]

    barrier = pltpu.get_barrier_semaphore()

    def greet(section, index):
        pl.semaphore_signal(barrier, inc=1, device_id=(section, index), device_id_type=MESH)

    greet(down, b)
    for dh in (3, 1, 0):
        for dx in range(4):
            if dx or dh:
                greet(s, at(dx, dh))

    def load(index, src, dst):
        copy = pltpu.make_async_copy(src, dst, cp_sem.at[index])
        copy.start()
        return copy

    small = [load(0, tok_hbm, tok_v), load(1, rank_hbm, rank_v), load(2, gates_hbm, gates_v)]
    got_rows = load(3, rows_hbm, x_v)
    got_pre = load(4, pre_hbm, pre_v)
    got_w = load(5, w_hbm, w_v)
    pl.semaphore_wait(barrier, 12)

    tok_copy = pltpu.make_async_remote_copy(
        tok_hbm, tokp_v, tok_sem.at[0], tok_sem.at[1], device_id=(up, b), device_id_type=MESH
    )
    tok_copy.start()

    got_rows.wait()
    tok_copy.wait()
    pl.semaphore_signal(far_sem, inc=1, device_id=(s, at(0, 3)), device_id_type=MESH)
    q = iota((slots, slots), 0)
    r = iota((slots, slots), 1)
    tokens_below = tokp_v[...]
    first = jnp.sum(onehot(tokens_below < b * shard), axis=1, keepdims=True).astype(jnp.int32)
    t = iota((shard, slots), 0)
    where_token = onehot(tokens_below - b * shard == t).astype(BF16)
    wide = iota((2 * NB, slots), 1)
    line = iota((2 * NB, slots), 0)
    later_below = jnp.where(wide - first >= NB, 1, 0)
    owner = onehot((lax.rem(wide, NB) == lax.rem(line, NB)) & (later_below == line // NB)).astype(BF16)
    select = dot(owner, where_token, NT).astype(BF16)
    a2a = {}

    def pick(c):
        picked = dot(select, x_v[:, c * cw:(c + 1) * cw], NN)
        for g in range(GROUPS):
            for k in range(2):
                place_v[pl.ds(2 * g + k, NB, stride=NB), :] = picked[k * NB:(k + 1) * NB, g * gw:(g + 1) * gw]
        sb_v[c] = place_v[...].astype(BF16)

    def deal(c, who):
        for i in who:
            to = everyone[i]
            copy = pltpu.make_async_remote_copy(
                sb_v.at[c, pl.ds(pl.multiple_of(to * NB, NB), NB)],
                r_v.at[c, pl.ds(pl.multiple_of(b * NB, NB), NB)],
                a2a_send.at[c * NB + i], a2a_recv.at[c * NB + i], device_id=(down, to), device_id_type=MESH,
            )
            copy.start()
            a2a[c, i] = copy

    far, near = range(4), range(4, NB)
    pick(0)
    for c in range(CHUNKS):
        pick(c)
        deal(c, near)
    pl.semaphore_wait(far_sem, 1)
    for c in range(CHUNKS):
        deal(c, far)

    for copy in small:
        copy.wait()
    tokens = tok_v[...]
    block = tokens // shard
    source = q // NB
    start = jnp.sum(onehot(block < source), axis=1, keepdims=True).astype(jnp.int32)
    later = jnp.where(r - start >= NB, 1, 0)
    found = onehot((block == source) & (later == lax.rem(q, 2))).astype(BF16)
    p = iota((GROUPS * per, slots), 0)
    wanted = onehot(iota((GROUPS * per, slots), 1) == lax.rem(p, per) * NB + b).astype(BF16)
    pack = dot(wanted, found, NT)
    same = (iota(pack.shape, 0) // per) == lax.rem(iota(pack.shape, 1), NB) // 2
    pack = jnp.where(same, pack, 0.0).astype(BF16)

    here = onehot(tokens - b * shard == t).astype(BF16)
    both = dot(gates_v[...], here, NN)
    part = jnp.where(rank_v[...] == 0, both[0:1, :], both[1:2, :])
    wp_v[b] = part

    def exchange(buffer, send, recv):
        started = []
        for i, to in enumerate(everyone[:-1]):
            copy = pltpu.make_async_remote_copy(
                buffer.at[b], buffer.at[b], send.at[i], recv.at[i], device_id=(s, to), device_id_type=MESH
            )
            copy.start()
            started.append(copy)
        return started

    weights = exchange(wp_v, wp_send, wp_recv)

    got_pre.wait()
    pf_v[...] = pre_v[...].astype(F32)
    tiles = units // 128
    stride = NB * 2 * tiles
    for o in range(NB):
        for c in range(tiles):
            gate = pf_v[pl.ds(2 * tiles * o + 2 * c, per, stride=stride), :]
            up_pre = pf_v[pl.ds(2 * tiles * o + 2 * c + 1, per, stride=stride), :]
            sig = jax.nn.sigmoid(gate)
            activated = gate * sig
            into = (pl.ds(o * per, per), pl.ds(c * 128, 128))
            act_v[into] = activated
            dgp_v[into] = up_pre * sig * (1.0 + gate * (1.0 - sig))
            hid_v[into] = (activated * up_pre).astype(BF16).astype(F32)

    rows = GROUPS * per
    started = {}

    def send(name, chunk, owner_blk, part, to):
        low, size = (0, rows) if part is None else (part * rows // 2, rows // 2)
        index = list(NAMES).index(name)
        ref = g_v.at[chunk, owner_blk, pl.ds(low, size)]
        copy = pltpu.make_async_remote_copy(
            ref, ref, ag_send.at[chunk * len(NAMES) + index], ag_recv.at[chunk * len(NAMES) + index],
            device_id=(s, to), device_id_type=MESH,
        )
        copy.start()
        started[name, chunk] = copy

    def arrived(name, chunk):
        started[name, chunk].wait_recv()

    def x_send(i, c):
        send(f"xo{i}", c, at(0, OFFSETS[i]), None, at(2, 0))
        send(f"x+{i}", c, at(0, OFFSETS[i]), None, at(1, 0))
        send(f"x-{i}", c, at(0, OFFSETS[i]), None, at(3, 0))

    def z_forward(c):
        arrived("z+", c)
        send("zf+", c, at(0, 3), 0, at(0, 1))
        arrived("z-", c)
        send("zf-", c, at(0, 1), 1, at(0, 3))
        x_send(1, c)
        x_send(2, c)

    def z_last(c):
        arrived("zf+", c)
        arrived("zf-", c)
        x_send(3, c)

    def multiply(c):
        for i in range(4):
            for kind in ("x+", "x-", "xo"):
                arrived(f"{kind}{i}", c)
        left = [g_v[c, :, g * per:(g + 1) * per, :].reshape(slots, gw) for g in range(GROUPS)]
        product = dot(jnp.concatenate(left, axis=1), w_v[:, c * cw:(c + 1) * cw], NT)
        dh_v[...] = product if c == 0 else dh_v[...] + product

    for c in range(CHUNKS):
        for i in range(NB):
            a2a[c, i].wait_recv()
        g_v[c, b] = dot(pack, r_v[c], NN).astype(BF16)
        send("z+", c, b, None, at(0, 1))
        send("z-", c, b, None, at(0, 3))
        x_send(0, c)
    z_forward(0)
    for copy in weights:
        copy.wait()
    weight_row = jnp.sum(wp_v[...], axis=0)
    in_place = r == lax.rem(q, per) * NB + q // per
    weight = jnp.sum(jnp.where(in_place, weight_row, 0.0), axis=1, keepdims=True)
    got_w.wait()
    for c in range(1, CHUNKS):
        z_forward(c)
    for c in range(CHUNKS):
        z_last(c)
    for c in range(CHUNKS):
        multiply(c)

    dh = dh_v[...]
    share = jnp.sum(hid_v[...] * dh, axis=1, keepdims=True)
    dg_v[b] = jnp.sum(jnp.where(in_place, share, 0.0), axis=0, keepdims=True)
    sums = exchange(dg_v, dg_send, dg_recv)

    grad = weight * dh
    d_gate_pre = grad * dgp_v[...]
    d_up = grad * act_v[...]
    for o in range(NB):
        for c in range(tiles):
            part = (slice(o * per, (o + 1) * per), slice(c * 128, (c + 1) * 128))
            pf_v[pl.ds(2 * tiles * o + 2 * c, per, stride=stride), :] = d_gate_pre[part]
            pf_v[pl.ds(2 * tiles * o + 2 * c + 1, per, stride=stride), :] = d_up[part]
    dpre_v[...] = pf_v[...].astype(BF16)
    put_pre = load(0, dpre_v, dpre_hbm)

    for copy in sums:
        copy.wait()
    total = dg_v[0]
    for i in range(1, NB):
        total += dg_v[i]
    dsum_v[...] = total
    put_gate = load(1, dsum_v, dgate_hbm)

    for copy in [*a2a.values(), *started.values()]:
        copy.wait_send()
    put_pre.wait()
    put_gate.wait()


def hand_on_kernel(dpre_ref, dgate_ref, dpre_out, dgate_out):
    dpre_out[...] = dpre_ref[...]
    dgate_out[...] = dgate_ref[...]


NAMES = ("z+", "z-", "zf+", "zf-") + tuple(f"{kind}{i}" for i in range(4) for kind in ("x+", "x-", "xo"))


def per_device(sections, sent_grad, gates, slot_token, slot_rank, pre_act, down_weight):
    rows, weight = sent_grad[0], down_weight[0]
    shard, width = rows.shape
    slots, _, units = pre_act.shape[1:]
    tiles = units // 128
    gw, per = width // CHUNKS // GROUPS, slots // NB
    pre = pre_act[0].reshape(slots, 2, tiles, 128).transpose(0, 2, 1, 3).reshape(slots * tiles * 2, 128)
    vmem = pl.BlockSpec(memory_space=pltpu.VMEM)
    hbm = pl.BlockSpec(memory_space=pl.ANY)
    dma = pltpu.SemaphoreType.DMA
    n_ag = CHUNKS * len(NAMES)
    d_pre, d_gate = pl.pallas_call(
        functools.partial(relay_kernel, sections),
        out_shape=(
            jax.ShapeDtypeStruct(pre.shape, BF16),
            jax.ShapeDtypeStruct((1, slots), F32),
        ),
        in_specs=[hbm] * 6,
        out_specs=(hbm, hbm),
        scratch_shapes=[
            pltpu.VMEM((slots, gw), F32),
            pltpu.VMEM((1, slots), jnp.int32),
            pltpu.VMEM((1, slots), jnp.int32),
            pltpu.VMEM((2, shard), BF16),
            pltpu.VMEM(pre.shape, BF16),
            pltpu.VMEM((1, slots), F32),
            pltpu.VMEM((shard, width), BF16),
            pltpu.VMEM(weight.shape, BF16),
            pltpu.VMEM(pre.shape, BF16),
            pltpu.VMEM((1, slots), jnp.int32),
            pltpu.VMEM((CHUNKS, slots, gw), BF16),
            pltpu.VMEM((CHUNKS, slots, gw), BF16),
            pltpu.VMEM((CHUNKS, NB, GROUPS * per, gw), BF16),
            pltpu.VMEM((NB, 1, slots), F32),
            pltpu.VMEM((NB, 1, slots), F32),
            pltpu.VMEM(pre.shape, F32),
            pltpu.VMEM((slots, units), F32),
            pltpu.VMEM((slots, units), F32),
            pltpu.VMEM((slots, units), F32),
            pltpu.VMEM((slots, units), F32),
            pltpu.SemaphoreType.REGULAR, dma((6,)), dma((2,)), dma((NB,)), dma((NB,)), dma((CHUNKS * NB,)), dma((CHUNKS * NB,)),
            dma((n_ag,)), dma((n_ag,)), dma((NB,)), dma((NB,)),
        ],
        compiler_params=pltpu.CompilerParams(
            collective_id=0, has_side_effects=True, vmem_limit_bytes=56 * 2**20
        ),
    )(slot_token, slot_rank, gates[0].T, rows, pre, weight)
    d_pre, d_gate = pl.pallas_call(
        hand_on_kernel,
        out_shape=(
            jax.ShapeDtypeStruct(pre.shape, BF16),
            jax.ShapeDtypeStruct((1, slots), F32),
        ),
        in_specs=[vmem, vmem],
        out_specs=(vmem, vmem),
    )(d_pre, d_gate)
    d_pre = d_pre.reshape(slots, tiles, 2, 128).transpose(0, 2, 1, 3).reshape(1, slots, 2, units)
    return d_pre, d_gate


def solution(mesh):
    placed = (
        P("section", "blk", None),
        P("section", "blk", None),
        P("section", None),
        P("section", None),
        P("section", None, None, "blk"),
        P("section", "blk", None),
    )
    return jax.shard_map(
        functools.partial(per_device, mesh.shape["section"]),
        mesh=mesh,
        in_specs=placed,
        out_specs=(P("section", None, None, "blk"), P("section", None)),
        check_vma=False,
    )
```
